256 devices in a mesh: fsdp: 128 (over x_lo, z, y, core), dp: 2 (over x_hi).
Axes of the slice: x: 4 (x_hi: 2, x_lo: 2; x = x_hi * 2 + x_lo), y: 4, z: 8, core: 2. Of those that a mesh axis runs over, the one named last changes fastest.
Arguments:
- inputs: bfloat16 [512, 256, 512], P(('fsdp', 'dp')), may hold values from -6 to 6
- memory: bfloat16 [512, 256, 512], P(('fsdp', 'dp')), may hold values from -6 to 6
- out_grad: bfloat16 [512, 256, 512], P(('fsdp', 'dp')), may hold values from -6 to 6
- weights: float32 [8192, 512], P('fsdp'), may hold values from -0.1659025 to 0.1659025
- first_moment: float32 [8192, 512], P('fsdp'), may hold values from -94.130055 to 94.130055
- second_moment: float32 [8192, 512], P('fsdp'), may hold values from 0 to 27525.12, as said below
- norms: float32 [6, 512], P(None, 'fsdp'), may hold values from -0.3 to 1.4
- norm_first: float32 [6, 512], P(None, 'fsdp'), may hold values from -123.09315 to 123.09315
- norm_second: float32 [6, 512], P(None, 'fsdp'), may hold values from 0 to 47185.92, as said below
Outputs:
- outputs: bfloat16 [512, 256, 512], P(('fsdp', 'dp'))
- grad_inputs: float32 [512, 256, 512], P(('fsdp', 'dp'))
- grad_memory: float32 [512, 256, 512], P(('fsdp', 'dp'))
- weight_grads: float32 [8192, 512], P('fsdp')
- new_weights: float32 [8192, 512], P('fsdp')
- new_second: float32 [8192, 512], P('fsdp')
- norm_grads: float32 [6, 512], P(None, 'fsdp')
- new_norms: float32 [6, 512], P(None, 'fsdp')
- new_norm_second: float32 [6, 512], P(None, 'fsdp')
The draws below stay inside these ranges and needn't reach their ends.
Inputs may be any that keep to these rules, and one draw needn't show every extreme that they name: `second_moment`: positive. `norm_second`: positive.
All inputs are finite; a program needn't handle non-finite values.
Results may differ from the reference program's by a relative error of at most 0.034.
The reference program's roundings to bfloat16 on the way count: a program that leaves them out, or rounds other values in their place, can miss the bound.
Values may be sent and summed in bfloat16 or wider, within the bound.
No kernel may reach another device: no remote copies, remote signals or barrier semaphores. Data moves between devices by JAX's collectives and lax.ppermute only.
A program may use at most 192 MiB of HBM per device.

```python
import math
import jax
import jax.numpy as jnp
from jax import lax

D = 512
HEADS = 8
HEAD = 64
FF = 2048
LEN = 256
STEP = 10
ROWS = 8192
SENTS = 512
TOKENS = 131072


def block_index():
    place = jnp.arange(ROWS)
    return jnp.where(place < 8 * D, place // D, jnp.where(place < 8 * D + FF, 8, 9))


def weight_scales():
    sharp = 1.42 * D ** (-0.5)
    drawn = D ** (-0.5)
    wide = max(1.0, (LEN / 55.0) ** 0.5) * D ** (-0.5)
    return jnp.array([sharp, sharp, drawn, wide, sharp, sharp, drawn, wide, drawn, FF ** (-0.5)], jnp.float32)


def grad_sizes():
    attn = 1.2
    output = 1.3 * min(1.0, (55.0 / LEN) ** 0.5)
    table = [attn, attn, attn, output, attn, attn, attn, output, 0.35, 0.7]
    return jnp.array(table, jnp.float32) * math.sqrt(TOKENS)


def norm_sizes():
    return jnp.array([1.7, 1.7, 1.2, 1.2, 0.7, 0.7], jnp.float32) * math.sqrt(TOKENS)


def draw_weights(key, part):
    key = jax.random.fold_in(key, 11)
    scale = weight_scales()[block_index()][:, None]
    return jax.random.uniform(key, (ROWS, D), jnp.float32, -1.7320508, 1.7320508) * scale


def draw_first_moment(key, part):
    key = jax.random.fold_in(key, 12)
    scale = grad_sizes()[block_index()][:, None]
    return jax.random.uniform(key, (ROWS, D), jnp.float32, -0.19, 0.19) * scale


def draw_second_moment(key, part):
    key = jax.random.fold_in(key, 13)
    scale = grad_sizes()[block_index()][:, None]
    factor = jnp.exp(jax.random.uniform(key, (ROWS, D), jnp.float32, math.log(0.7), math.log(6.0)))
    return 0.0204 * factor * scale * scale


def draw_norms(key, part):
    key = jax.random.fold_in(key, 14)
    base = jax.random.uniform(key, (6, D), jnp.float32, -1.0, 1.0)
    row_kind = (jnp.arange(6) % 2)[:, None]
    return jnp.where(row_kind == 0, 1.0 + 0.4 * base, 0.3 * base)


def draw_norm_first(key, part):
    key = jax.random.fold_in(key, 15)
    scale = norm_sizes()[:, None]
    return jax.random.uniform(key, (6, D), jnp.float32, -0.19, 0.19) * scale


def draw_norm_second(key, part):
    key = jax.random.fold_in(key, 16)
    scale = norm_sizes()[:, None]
    factor = jnp.exp(jax.random.uniform(key, (6, D), jnp.float32, math.log(0.7), math.log(6.0)))
    return 0.0204 * factor * scale * scale


def block_scale(stream_key, shape, pieces, low, top_value):
    level = 1.0
    for position, shards_of in pieces:
        draws = jax.random.uniform(jax.random.fold_in(jax.random.fold_in(stream_key, 6), position), (shards_of,), jnp.float32, low / len(pieces), top_value / len(pieces))
        level = level * jnp.repeat(jnp.exp(draws), shape[position] // shards_of).reshape((-1,) + (1,) * (len(shape) - 1 - position))
    return level


def bell_draw(rng, extent, deviation, reach, cuts=(), held_as=jnp.bfloat16):
    values = deviation * jax.random.normal(rng, extent, jnp.float32)
    if cuts:
        values = values * block_scale(rng, extent, cuts, -0.22, 0.18)
    return jnp.clip(values, -reach, reach).astype(held_as)


def setup_inputs(seed: int = 0) -> dict:
    key_of = jax.random.split(jax.random.key(seed), 10)
    return {
        "inputs": bell_draw(key_of[0], (SENTS, LEN, D), 1.0, 6.0, ((0, 256),)),
        "memory": bell_draw(key_of[1], (SENTS, LEN, D), 1.0, 6.0, ((0, 256),)),
        "out_grad": bell_draw(key_of[2], (SENTS, LEN, D), 1.0, 6.0, ((0, 256),)),
        "weights": draw_weights(jax.random.fold_in(key_of[9], 71), 0),
        "first_moment": draw_first_moment(jax.random.fold_in(key_of[9], 71), 0),
        "second_moment": draw_second_moment(jax.random.fold_in(key_of[9], 71), 0),
        "norms": draw_norms(jax.random.fold_in(key_of[9], 71), 0),
        "norm_first": draw_norm_first(jax.random.fold_in(key_of[9], 71), 0),
        "norm_second": draw_norm_second(jax.random.fold_in(key_of[9], 71), 0),
    }


@jax.custom_vjp
def low(v):
    return lax.optimization_barrier(v.astype(jnp.bfloat16)).astype(jnp.float32)

@jax.custom_vjp
def low_back(v):
    return v

def low_keep(v):
    return (low(v), None)

def low_pass(kept, grad):
    return (grad,)

def back_keep(v):
    return (v, None)

def back_low(kept, grad):
    return (low(grad),)
low.defvjp(low_keep, low_pass)
low_back.defvjp(back_keep, back_low)
EPS_NORM = 1e-05
BETA_ONE = 0.9
BETA_TWO = 0.98
RATE = 0.1
RATE_NORM = 0.4
DECAY = 0.01
EPS_ADAM = 1e-09

def matmul(former, latter):
    return jnp.dot(former, latter, precision=lax.Precision.HIGHEST, preferred_element_type=jnp.float32)

def rounded_both(vector):
    return low(low_back(vector))

def layer_norm(vector, gain_row, shift_row):
    centre = vector - lax.optimization_barrier(jnp.mean(vector, axis=-1, keepdims=True))
    spread = lax.optimization_barrier(jnp.mean(centre * centre, axis=-1, keepdims=True))
    return centre * lax.rsqrt(spread + EPS_NORM) * gain_row + shift_row

def attend(queries, key_rows, values, w_out):
    length = queries.shape[0]
    span = key_rows.shape[0]
    query_heads = queries.reshape(length, HEADS, HEAD)
    key_heads = key_rows.reshape(span, HEADS, HEAD)
    value_heads = values.reshape(span, HEADS, HEAD)
    scores = jnp.einsum('qhe,khe->hqk', query_heads, key_heads, precision=lax.Precision.HIGHEST) * HEAD ** (-0.5)
    scores = low_back(scores)
    weights_soft = low(jax.nn.softmax(scores, axis=-1))
    mixture = jnp.einsum('hqk,khe->qhe', weights_soft, value_heads, precision=lax.Precision.HIGHEST)
    mixture = rounded_both(mixture.reshape(length, HEADS * HEAD))
    return low_back(matmul(mixture, w_out))

def sentence_layer(low_weights, low_norms, start, memory_row):
    blocks = [low_weights[block * D:(block + 1) * D] for block in range(8)]
    w_in = low_weights[8 * D:8 * D + FF]
    w_down = low_weights[8 * D + FF:]
    first_in = low(layer_norm(start, low_norms[0], low_norms[1]))
    queries = rounded_both(matmul(first_in, blocks[0]))
    key_rows = rounded_both(matmul(first_in, blocks[1]))
    values = rounded_both(matmul(first_in, blocks[2]))
    after_one = start + attend(queries, key_rows, values, blocks[3])
    second_in = low(layer_norm(after_one, low_norms[2], low_norms[3]))
    cross_query = rounded_both(matmul(second_in, blocks[4]))
    cross_keys = rounded_both(matmul(memory_row, blocks[5]))
    cross_values = rounded_both(matmul(memory_row, blocks[6]))
    after_two = after_one + attend(cross_query, cross_keys, cross_values, blocks[7])
    third_in = low(layer_norm(after_two, low_norms[4], low_norms[5]))
    up_proj = low_back(matmul(third_in, w_in.T))
    active = low(jax.nn.silu(up_proj))
    return after_two + low_back(matmul(active, w_down))

def adam_update(param, first, second, grad, rate):
    first_new = BETA_ONE * first + (1.0 - BETA_ONE) * grad
    second_new = BETA_TWO * second + (1.0 - BETA_TWO) * grad * grad
    fix_one = 1.0 - BETA_ONE ** STEP
    fix_two = 1.0 - BETA_TWO ** STEP
    update = first_new / fix_one / (jnp.sqrt(second_new / fix_two) + EPS_ADAM)
    return (param - rate * (update + DECAY * param), second_new)

def reference(inputs, memory, out_grad, weights, first_moment, second_moment, norms, norm_first, norm_second):
    inputs_wide = inputs.astype(jnp.float32)
    memory_wide = memory.astype(jnp.float32)
    cotangent = out_grad.astype(jnp.float32)

    def forward(weight_in, norm_in, start_all, memory_all):
        low_weights = low(weight_in)
        low_norms = low(norm_in)
        per_sentence = jax.checkpoint(lambda pair: sentence_layer(low_weights, low_norms, pair[0], pair[1]))
        return lax.map(per_sentence, (start_all, memory_all))
    result, pullback = jax.vjp(forward, weights, norms, inputs_wide, memory_wide)
    grad_w, grad_n, grad_x, grad_m = pullback(cotangent)
    new_w, second_w = adam_update(weights, first_moment, second_moment, grad_w, RATE)
    new_n, second_n = adam_update(norms, norm_first, norm_second, grad_n, RATE_NORM)
    return (result.astype(jnp.bfloat16), grad_x, grad_m, grad_w, new_w, second_w, grad_n, new_n, second_n)
```

```python
import jax
import jax.numpy as jnp
from jax import lax
from jax.sharding import PartitionSpec as P

HEADS = 8
STEP = 10


EPS_NORM = 1e-05
BETA_ONE = 0.9
BETA_TWO = 0.98
RATE = 0.1
RATE_NORM = 0.4
DECAY = 0.01
EPS_ADAM = 1e-09


def product(former, latter):
    return jnp.dot(former, latter, preferred_element_type=jnp.float32)


def left_product(former, latter):
    return lax.dot_general(
        former, latter, (((0,), (0,)), ((), ())), preferred_element_type=jnp.float32
    )


def right_product(former, latter):
    return lax.dot_general(
        former, latter, (((1,), (1,)), ((), ())), preferred_element_type=jnp.float32
    )


def layer_norm(vector, gain_row, shift_row):
    centre = vector - jnp.mean(vector, axis=-1, keepdims=True)
    factor = lax.rsqrt(jnp.mean(centre * centre, axis=-1, keepdims=True) + EPS_NORM)
    normed = centre * factor
    return (normed * gain_row + shift_row, normed, factor)


def norm_back(grad_out, normed, factor, gain_row):
    scaled = grad_out * gain_row
    mean_one = jnp.mean(scaled, axis=-1, keepdims=True)
    mean_two = jnp.mean(scaled * normed, axis=-1, keepdims=True)
    grad_in = factor * (scaled - mean_one - normed * mean_two)
    return (grad_in, jnp.sum(grad_out * normed, axis=0), jnp.sum(grad_out, axis=0))


def split_heads(vector):
    return vector.reshape(vector.shape[0], HEADS, vector.shape[1] // HEADS)


def attention_scores(queries, key_rows):
    factor = (queries.shape[1] // HEADS) ** (-0.5)
    return (
        jnp.einsum(
            "qhe,khe->hqk",
            split_heads(queries),
            split_heads(key_rows),
            preferred_element_type=jnp.float32,
        )
        * factor
    )


def attend_forward(queries, key_rows, values):
    scores = attention_scores(queries, key_rows)
    highest = jnp.max(scores, axis=-1, keepdims=True)
    raised = jnp.exp(scores - highest)
    summed = jnp.sum(raised, axis=-1, keepdims=True)
    soft_low = (raised / summed).astype(jnp.bfloat16)
    mixture = jnp.einsum(
        "hqk,khe->qhe", soft_low, split_heads(values), preferred_element_type=jnp.float32
    )
    return (mixture.reshape(queries.shape).astype(jnp.bfloat16), highest + jnp.log(summed))


def attend_back(queries, key_rows, values, log_total, grad_mix):
    factor = (queries.shape[1] // HEADS) ** (-0.5)
    scores = attention_scores(queries, key_rows)
    softmax_rows = jnp.exp(scores - log_total)
    heads_grad = split_heads(grad_mix)
    grad_values = jnp.einsum(
        "hqk,qhe->khe",
        softmax_rows.astype(jnp.bfloat16),
        heads_grad,
        preferred_element_type=jnp.float32,
    )
    grad_soft = jnp.einsum(
        "qhe,khe->hqk", heads_grad, split_heads(values), preferred_element_type=jnp.float32
    )
    inner = jnp.sum(softmax_rows * grad_soft, axis=-1, keepdims=True)
    grad_scores = (softmax_rows * (grad_soft - inner)).astype(jnp.bfloat16)
    grad_query = (
        jnp.einsum(
            "hqk,khe->qhe", grad_scores, split_heads(key_rows), preferred_element_type=jnp.float32
        )
        * factor
    )
    grad_keys = (
        jnp.einsum(
            "hqk,qhe->khe", grad_scores, split_heads(queries), preferred_element_type=jnp.float32
        )
        * factor
    )
    return (
        grad_query.reshape(queries.shape).astype(jnp.bfloat16),
        grad_keys.reshape(key_rows.shape).astype(jnp.bfloat16),
        grad_values.reshape(values.shape).astype(jnp.bfloat16),
    )


def unpack(full_w, model_width):
    hidden = (full_w.shape[0] - 8 * model_width) // 2
    matrices = [full_w[block * model_width : (block + 1) * model_width] for block in range(8)]
    w_in = full_w[8 * model_width : 8 * model_width + hidden]
    w_down = full_w[8 * model_width + hidden :]
    return (matrices, w_in, w_down)


def forward_pass(inputs_row, memory_row, full_w, full_n):
    matrices, w_in, w_down = unpack(full_w, inputs_row.shape[1])
    norm_rows = full_n.astype(jnp.float32)
    block_input = inputs_row.astype(jnp.float32)
    stored = {}
    normal_one, stored["normed_one"], stored["factor_one"] = layer_norm(
        block_input, norm_rows[0], norm_rows[1]
    )
    first_in = normal_one.astype(jnp.bfloat16)
    stored["first_in"] = first_in
    stored["query_one"] = product(first_in, matrices[0]).astype(jnp.bfloat16)
    stored["key_one"] = product(first_in, matrices[1]).astype(jnp.bfloat16)
    stored["value_one"] = product(first_in, matrices[2]).astype(jnp.bfloat16)
    stored["mix_one"], stored["log_one"] = attend_forward(
        stored["query_one"], stored["key_one"], stored["value_one"]
    )
    after_one = block_input + product(stored["mix_one"], matrices[3])
    normal_two, stored["normed_two"], stored["factor_two"] = layer_norm(
        after_one, norm_rows[2], norm_rows[3]
    )
    second_in = normal_two.astype(jnp.bfloat16)
    stored["second_in"] = second_in
    stored["query_two"] = product(second_in, matrices[4]).astype(jnp.bfloat16)
    stored["key_two"] = product(memory_row, matrices[5]).astype(jnp.bfloat16)
    stored["value_two"] = product(memory_row, matrices[6]).astype(jnp.bfloat16)
    stored["mix_two"], stored["log_two"] = attend_forward(
        stored["query_two"], stored["key_two"], stored["value_two"]
    )
    after_two = after_one + product(stored["mix_two"], matrices[7])
    normal_three, stored["normed_three"], stored["factor_three"] = layer_norm(
        after_two, norm_rows[4], norm_rows[5]
    )
    third_in = normal_three.astype(jnp.bfloat16)
    stored["third_in"] = third_in
    up_proj = right_product(third_in, w_in)
    stored["up_proj"] = up_proj
    active = jax.nn.silu(up_proj).astype(jnp.bfloat16)
    stored["active"] = active
    result = after_two + product(active, w_down)
    return (stored, result)


def backward_pass(stored, grad_low, memory_row, full_w, full_n):
    matrices, w_in, w_down = unpack(full_w, grad_low.shape[1])
    norm_rows = full_n.astype(jnp.float32)
    grad_out = grad_low.astype(jnp.float32)
    grad_down = left_product(stored["active"], grad_low)
    grad_act = right_product(grad_low, w_down)
    up_proj = stored["up_proj"]
    sigma = jax.nn.sigmoid(up_proj)
    grad_up = (grad_act * sigma * (1.0 + up_proj * (1.0 - sigma))).astype(jnp.bfloat16)
    grad_inw = left_product(grad_up, stored["third_in"])
    back_three, gain_three, bias_three = norm_back(
        product(grad_up, w_in), stored["normed_three"], stored["factor_three"], norm_rows[4]
    )
    grad_two = grad_out + back_three
    cross_out = grad_two.astype(jnp.bfloat16)
    grad_woc = left_product(stored["mix_two"], cross_out)
    cross_mix = right_product(cross_out, matrices[7]).astype(jnp.bfloat16)
    grad_qc, grad_kc, grad_vc = attend_back(
        stored["query_two"], stored["key_two"], stored["value_two"], stored["log_two"], cross_mix
    )
    grad_wqc = left_product(stored["second_in"], grad_qc)
    grad_wkc = left_product(memory_row, grad_kc)
    grad_wvc = left_product(memory_row, grad_vc)
    grad_memory = right_product(grad_kc, matrices[5]) + right_product(grad_vc, matrices[6])
    back_two, gain_two, bias_two = norm_back(
        right_product(grad_qc, matrices[4]),
        stored["normed_two"],
        stored["factor_two"],
        norm_rows[2],
    )
    grad_one = grad_two + back_two
    self_out = grad_one.astype(jnp.bfloat16)
    grad_wo = left_product(stored["mix_one"], self_out)
    self_mix = right_product(self_out, matrices[3]).astype(jnp.bfloat16)
    grad_q, grad_k, grad_v = attend_back(
        stored["query_one"], stored["key_one"], stored["value_one"], stored["log_one"], self_mix
    )
    grad_wq = left_product(stored["first_in"], grad_q)
    grad_wk = left_product(stored["first_in"], grad_k)
    grad_wv = left_product(stored["first_in"], grad_v)
    grad_first = (
        right_product(grad_q, matrices[0])
        + right_product(grad_k, matrices[1])
        + right_product(grad_v, matrices[2])
    )
    back_one, gain_one, bias_one = norm_back(
        grad_first, stored["normed_one"], stored["factor_one"], norm_rows[0]
    )
    grad_start = grad_one + back_one
    weight_term = jnp.concatenate(
        [
            grad_wq,
            grad_wk,
            grad_wv,
            grad_wo,
            grad_wqc,
            grad_wkc,
            grad_wvc,
            grad_woc,
            grad_inw,
            grad_down,
        ],
        axis=0,
    )
    norm_term = jnp.stack([gain_one, bias_one, gain_two, bias_two, gain_three, bias_three])
    return (grad_start, grad_memory, weight_term, norm_term)


def adam_update(param, first, second, grad, rate):
    first_new = BETA_ONE * first + (1.0 - BETA_ONE) * grad
    second_new = BETA_TWO * second + (1.0 - BETA_TWO) * grad * grad
    fix_one = 1.0 - BETA_ONE**STEP
    fix_two = 1.0 - BETA_TWO**STEP
    update = first_new / fix_one / (jnp.sqrt(second_new / fix_two) + EPS_ADAM)
    return (param - rate * (update + DECAY * param), second_new)


def exchange(block, axis):
    return lax.ppermute(block, axis, [(0, 1), (1, 0)])


def spread(block, axis, count):
    return lax.all_to_all(
        jnp.broadcast_to(block[None], (count,) + block.shape), axis, 0, 0, tiled=True
    )


def in_order(own, other, place):
    first = jnp.where(place == 0, own, other)
    second = jnp.where(place == 0, other, own)
    return first, second


def gather_parameters(shard_w, shard_n):
    along_x, along_core = lax.axis_index("xlo"), lax.axis_index("core")
    rows, width = shard_w.shape
    norm_row = jnp.pad(shard_n.reshape(1, -1), ((0, 7), (0, width - shard_n.size)))
    own = jnp.concatenate([shard_w, norm_row])
    attn, feed = in_order(own, exchange(own, "xlo"), along_x)
    norm_row = jnp.concatenate([attn[rows : rows + 1, :24], feed[rows : rows + 1, :24]], axis=1)
    norm_row = jnp.pad(norm_row, ((0, 7), (0, width - 48)))
    attn_z = spread(jnp.concatenate([attn[:rows], norm_row]), "z", 8)
    feed_z = spread(feed[:rows], "z", 8)
    norm_row = jnp.pad(attn_z[:, rows, :48].reshape(1, -1), ((0, 7), (0, width - 384)))
    attn_y = spread(jnp.concatenate([attn_z[:, :rows].reshape(8 * rows, width), norm_row]), "y", 4)
    feed_y = spread(feed_z.reshape(8 * rows, width), "y", 4)
    attn_c = jnp.stack(in_order(attn_y, exchange(attn_y, "core"), along_core))
    feed_c = jnp.stack(in_order(feed_y, exchange(feed_y, "core"), along_core))
    norms = attn_c[:, :, 8 * rows, :384].reshape(2, 4, 8, 2, 6, 4)
    norms = norms.transpose(4, 3, 2, 1, 0, 5).reshape(6, width)

    def whole(part):
        return part.reshape(2, 4, 8, rows, width).transpose(2, 1, 0, 3, 4).reshape(64 * rows, width)

    return jnp.concatenate([whole(attn_c[:, :, : 8 * rows]), whole(feed_c)]), norms


def pick(block, place):
    return lax.dynamic_index_in_dim(block, place, 0, keepdims=False)


def summed(block, axis, count):
    moved = lax.all_to_all(block, axis, 0, 0, tiled=True)
    return moved.reshape((count, -1) + block.shape[1:]).astype(jnp.float32).sum(0)


def scatter_gradients(grad_w, grad_n):
    low = jnp.bfloat16
    along_x, along_core = lax.axis_index("xlo"), lax.axis_index("core")
    rows, width = grad_w.shape[0] // 128, grad_w.shape[1]
    parts = grad_w.reshape(2, 8, 4, 2, rows, width).transpose(3, 0, 2, 1, 4, 5)
    norms = jnp.pad(grad_n, ((0, 2), (0, 0)))
    keep = pick(parts, along_core)
    sent = pick(parts, 1 - along_core).astype(low)
    keep = keep + exchange(sent, "core").astype(jnp.float32)
    norms = norms + exchange(norms.astype(low), "core").astype(jnp.float32)

    def with_norms(block, lines):
        lines = jnp.broadcast_to(lines[None], (block.shape[0], 8, width))
        return jnp.concatenate([block, lines], axis=1).astype(low)

    sums = []
    for part in range(2):
        block = keep[part].reshape(4, 8 * rows, width)
        if part == 0:
            block = with_norms(block, norms)
            block = summed(block, "y", 4)[0]
            norms = block[8 * rows :]
            block = with_norms(block[: 8 * rows].reshape(8, rows, width), norms)
            block = summed(block, "z", 8)[0]
            norms = block[rows:]
            sums.append(block[:rows])
        else:
            block = summed(block.astype(low), "y", 4)[0]
            block = summed(block.reshape(8, rows, width).astype(low), "z", 8)[0]
            sums.append(block)
    block = with_norms(jnp.stack(sums + sums), norms)
    block = summed(block, ("xhi", "xlo"), 4)[0]
    return block[:rows], block[rows : rows + 6]


def local(
    inputs, memory, out_grad, weights, first_moment, second_moment, norms, norm_first, norm_second
):
    full_w, full_n = gather_parameters(weights.astype(jnp.bfloat16), norms.astype(jnp.bfloat16))
    grad_w = 0.0
    grad_n = 0.0
    results = []
    grads_start = []
    grads_memory = []
    for sentence in range(inputs.shape[0]):
        stored, result = forward_pass(inputs[sentence], memory[sentence], full_w, full_n)
        grad_start, grad_mem, weight_term, norm_term = backward_pass(
            stored, out_grad[sentence], memory[sentence], full_w, full_n
        )
        results.append(result)
        grads_start.append(grad_start)
        grads_memory.append(grad_mem)
        grad_w = grad_w + weight_term
        grad_n = grad_n + norm_term
    owned_w, all_n = scatter_gradients(grad_w, grad_n)
    place = lax.axis_index(("xlo", "z", "y", "core"))
    owned_n = lax.dynamic_slice_in_dim(all_n, place * 4, 4, axis=1)
    new_w, second_w = adam_update(weights, first_moment, second_moment, owned_w, RATE)
    new_n, second_n = adam_update(norms, norm_first, norm_second, owned_n, RATE_NORM)
    outputs = jnp.stack(results).astype(jnp.bfloat16)
    return (
        outputs,
        jnp.stack(grads_start),
        jnp.stack(grads_memory),
        owned_w,
        new_w,
        second_w,
        owned_n,
        new_n,
        second_n,
    )


def solution(mesh):
    fsdp = ("xlo", "z", "y", "core")
    torus = jax.sharding.Mesh(mesh.devices.reshape(2, 8, 4, 2, 2), fsdp + ("xhi",))
    sentences = P(fsdp + ("xhi",), None, None)
    rows = P(fsdp, None)
    columns = P(None, fsdp)
    return jax.shard_map(
        local,
        mesh=torus,
        in_specs=(sentences,) * 3 + (rows,) * 3 + (columns,) * 3,
        out_specs=(sentences,) * 3 + (rows,) * 3 + (columns,) * 3,
        check_vma=False,
    )
```

```python
import jax
import jax.numpy as jnp
from jax import lax
from jax.experimental import pallas as pl
from jax.experimental.pallas import tpu as pltpu
from jax.sharding import PartitionSpec as P

LOW = jnp.bfloat16
WIDE = jnp.float32
HEADS = 8
HEAD = 64
LEN = 256
D = 512
FF = 2048
TOK = 512
EPS_NORM = 1e-05


def dot(former, latter, left, right):
    return lax.dot_general(
        former, latter, (((left,), (right,)), ((), ())), preferred_element_type=WIDE
    )


def nn(former, latter):
    return dot(former, latter, 1, 0)


def nt(former, latter):
    return dot(former, latter, 1, 1)


def tn(former, latter):
    return dot(former, latter, 0, 0)


def normalise(vector):
    centre = vector - jnp.mean(vector, axis=-1, keepdims=True)
    factor = lax.rsqrt(jnp.mean(centre * centre, axis=-1, keepdims=True) + EPS_NORM)
    return centre * factor, factor


def norm_back(grad, normed, factor, gain):
    scaled = grad * gain
    mean_one = jnp.mean(scaled, axis=-1, keepdims=True)
    mean_two = jnp.mean(scaled * normed, axis=-1, keepdims=True)
    return (
        factor * (scaled - mean_one - normed * mean_two),
        jnp.sum(grad * normed, axis=0, keepdims=True),
        jnp.sum(grad, axis=0, keepdims=True),
    )


def half_mask(which):
    lane = lax.broadcasted_iota(jnp.int32, (LEN, 128), 1)
    return (lane >= 64) if which else (lane < 64)


def attend(q_ref, k_ref, v_ref, prob_ref, mixed_ref):
    masks = [half_mask(0), half_mask(1)]
    zero = jnp.zeros((LEN, 128), LOW)
    for s in range(2):
        rows = pl.ds(s * LEN, LEN)
        for pair in range(4):
            cols = pl.ds(pair * 128, 128)
            queries, keys = q_ref[rows, cols], k_ref[rows, cols]
            values = v_ref[rows, cols].T
            for j in range(2):
                scores = nt(jnp.where(masks[j], keys, zero), queries)
                top = jnp.max(scores, axis=0, keepdims=True)
                raised = jnp.exp(scores - top)
                total = jnp.sum(raised, axis=0, keepdims=True)
                soft = (raised * (1.0 / total)).astype(LOW)
                prob_ref[s * 8 + pair * 2 + j] = soft
                mixed = nn(values[j * 64 : (j + 1) * 64], soft)
                mixed_ref[s, pl.ds(pair * 128 + j * 64, 64)] = mixed.astype(LOW)


def attend_back(q_ref, k_ref, v_ref, prob_ref, go_ref, dq_ref, dk_ref, dv_ref):
    masks = [half_mask(0), half_mask(1)]
    zero = jnp.zeros((LEN, 128), LOW)
    for s in range(2):
        rows = pl.ds(s * LEN, LEN)
        for pair in range(4):
            cols = pl.ds(pair * 128, 128)
            queries, keys, values = q_ref[rows, cols], k_ref[rows, cols], v_ref[rows, cols]
            grad_out = go_ref[rows, cols]
            keys_t = keys.T
            parts_q, parts_k, parts_v = [], [], []
            for j in range(2):
                soft = prob_ref[s * 8 + pair * 2 + j]
                grad_soft = nt(jnp.where(masks[j], values, zero), grad_out)
                wide = soft.astype(WIDE)
                weighed = wide * grad_soft
                inner = jnp.sum(weighed, axis=0, keepdims=True)
                grad_scores = (weighed - wide * inner).astype(LOW)
                parts_v.append(nn(soft, grad_out))
                parts_k.append(nn(grad_scores, queries))
                parts_q.append(nn(keys_t[j * 64 : (j + 1) * 64], grad_scores))
            dv_ref[rows, cols] = jnp.where(masks[0], parts_v[0], parts_v[1]).astype(LOW)
            dk_ref[rows, cols] = jnp.where(masks[0], parts_k[0], parts_k[1]).astype(LOW)
            grad_q = jnp.concatenate(parts_q, axis=0) * HEAD ** (-0.5)
            dq_ref[rows, cols] = grad_q.astype(LOW).T


def weight_copies(core, own, oth, held, sem, first, count):
    copies = []
    for place, source in ((core, own), (1 - core, oth)):
        for y in range(4):
            for b in range(count):
                copies.append(
                    pltpu.make_async_copy(
                        source.at[y, pl.ds((first + b) * 64, 64)], held.at[b, y, place], sem
                    )
                )
    for copy in copies:
        copy.start()
    return copies


def wait_all(copies):
    for copy in copies:
        copy.wait()


def block(held, b):
    return held[b].reshape(D, D)


def self_forward(core_ref, x_ref, own, oth, q, k, v, prob, mixed, after, norms, held, pieces, sem):
    core = core_ref[0]
    copies = []
    for place, source in ((0, own), (1, oth)):
        for y in range(4):
            copies.append(
                pltpu.make_async_copy(
                    source.at[y, pl.ds(512, 16)], pieces.at[place * 4 + y], sem.at[0]
                )
            )
    for copy in copies:
        copy.start()
    weights = weight_copies(core, own, oth, held, sem.at[1], 0, 4)
    start = x_ref[...].astype(WIDE)
    normed, _ = normalise(start)
    wait_all(copies)
    rows = jnp.sum(pieces[...].astype(WIDE), axis=0)
    norms[...] = rows[:8]
    first_in = (normed * rows[0:1] + rows[1:2]).astype(LOW)
    wait_all(weights)
    q[...] = nn(first_in, block(held, 0)).astype(LOW) * LOW(HEAD ** (-0.5))
    k[...] = nn(first_in, block(held, 1)).astype(LOW)
    v[...] = nn(first_in, block(held, 2)).astype(LOW)
    attend(q, k, v, prob, mixed)
    for s in range(2):
        lines = pl.ds(s * LEN, LEN)
        after[lines, :] = x_ref[lines, :].astype(WIDE) + tn(mixed[s], block(held, 3))


def cross_forward(core_ref, x_ref, m_ref, n_ref, own, oth, q, k, v, prob, mixed, after, held, sem):
    core = core_ref[0]
    weights = weight_copies(core, own, oth, held, sem.at[0], 4, 4)
    normed, _ = normalise(x_ref[...])
    second_in = (normed * n_ref[2:3] + n_ref[3:4]).astype(LOW)
    wait_all(weights)
    q[...] = nn(second_in, block(held, 0)).astype(LOW) * LOW(HEAD ** (-0.5))
    k[...] = nn(m_ref[...], block(held, 1)).astype(LOW)
    v[...] = nn(m_ref[...], block(held, 2)).astype(LOW)
    attend(q, k, v, prob, mixed)
    for s in range(2):
        lines = pl.ds(s * LEN, LEN)
        after[lines, :] = x_ref[lines, :] + tn(mixed[s], block(held, 3))


def store_grad(grads, place, core, b, value):
    parts = value.astype(LOW).reshape(4, 2, 64, D)
    for c in range(2):
        grads[lax.rem(core + c, 2), :, b] = parts[:, c]


def feed_both(core_ref, x_ref, g_ref, n_ref, own, oth, result, back, kept, sent, rows_out,
              held_in, held_down, grads, sem):
    core = core_ref[0]
    weights = [
        (
            weight_copies(core, own, oth, held_in.at[pl.ds(c, 1)], sem.at[c], c, 1),
            weight_copies(core, own, oth, held_down.at[pl.ds(c, 1)], sem.at[c + 4], 4 + c, 1),
        )
        for c in range(4)
    ]
    start = x_ref[...]
    normed, factor = normalise(start)
    third_in = (normed * n_ref[4:5] + n_ref[5:6]).astype(LOW)
    grad_low = g_ref[...]
    forward = start
    grad_in = jnp.zeros((TOK, D), WIDE)
    for c in range(4):
        wait_all(weights[c][0])
        w_in = block(held_in, c)
        up = nt(third_in, w_in)
        wait_all(weights[c][1])
        w_down = block(held_down, c)
        grad_act = nt(grad_low, w_down)
        sigma = 1.0 / (1.0 + jnp.exp(-up))
        active = up * sigma
        grad_up = (grad_act * (sigma + active * (1.0 - sigma))).astype(LOW)
        active = active.astype(LOW)
        forward = forward + nn(active, w_down)
        grad_in = grad_in + nn(grad_up, w_in)
        store_grad(grads, 0, core, c, tn(grad_up, third_in))
        store_grad(grads, 0, core, 4 + c, tn(active, grad_low))
    result[...] = forward.astype(LOW)
    first = pltpu.make_async_copy(grads.at[0], kept, sem.at[8])
    second = pltpu.make_async_copy(grads.at[1], sent, sem.at[9])
    second.start()
    first.start()
    grad, gain, bias = norm_back(grad_in, normed, factor, n_ref[4:5])
    back[...] = grad_low.astype(WIDE) + grad
    rows_out[...] = jnp.concatenate([gain, bias, jnp.zeros((6, D), WIDE)])
    second.wait()
    first.wait()


def cross_back(core_ref, d_ref, x_ref, m_ref, n_ref, own, oth, q, k, v, prob, mixed, back, dk, dv,
               kept, sent, rows_out, held, go, dq, grads, sem):
    core = core_ref[0]
    weights = weight_copies(core, own, oth, held, sem.at[0], 4, 4)
    down = d_ref[...].astype(LOW)
    wait_all(weights)
    go[...] = nt(down, block(held, 3)).astype(LOW)
    total = nn(mixed[0], down[:LEN]) + nn(mixed[1], down[LEN:])
    store_grad(grads, 0, core, 3, total)
    attend_back(q, k, v, prob, go, dq, dk, dv)
    normed, factor = normalise(x_ref[...])
    second_in = (normed * n_ref[2:3] + n_ref[3:4]).astype(LOW)
    grad_in = nt(dq[...], block(held, 0))
    store_grad(grads, 0, core, 0, tn(second_in, dq[...]))
    memory = m_ref[...]
    store_grad(grads, 0, core, 1, tn(memory, dk[...]))
    store_grad(grads, 0, core, 2, tn(memory, dv[...]))
    first = pltpu.make_async_copy(grads.at[0], kept, sem.at[1])
    second = pltpu.make_async_copy(grads.at[1], sent, sem.at[2])
    second.start()
    first.start()
    grad, gain, bias = norm_back(grad_in, normed, factor, n_ref[2:3])
    back[...] = d_ref[...] + grad
    rows_out[...] = jnp.concatenate([gain, bias, jnp.zeros((6, D), WIDE)])
    second.wait()
    first.wait()


def self_back(core_ref, d_ref, x_ref, n_ref, own, oth, q, k, v, prob, mixed, dq, dk, dv,
              kept, sent, held, go, grads, sem):
    core = core_ref[0]
    weights = weight_copies(core, own, oth, held, sem.at[0], 3, 1)
    down = d_ref[...].astype(LOW)
    wait_all(weights)
    go[...] = nt(down, block(held, 0)).astype(LOW)
    total = nn(mixed[0], down[:LEN]) + nn(mixed[1], down[LEN:])
    store_grad(grads, 0, core, 3, total)
    attend_back(q, k, v, prob, go, dq, dk, dv)
    normed, factor = normalise(x_ref[...].astype(WIDE))
    first_in = (normed * n_ref[0:1] + n_ref[1:2]).astype(LOW)
    store_grad(grads, 0, core, 0, tn(first_in, dq[...]))
    store_grad(grads, 0, core, 1, tn(first_in, dk[...]))
    store_grad(grads, 0, core, 2, tn(first_in, dv[...]))
    first = pltpu.make_async_copy(grads.at[0], kept, sem.at[1])
    second = pltpu.make_async_copy(grads.at[1], sent, sem.at[2])
    second.start()
    first.start()
    second.wait()
    first.wait()


def last_back(core_ref, d_ref, x_ref, n_ref, own, oth, dq, dk, dv, dkc, dvc, back, back_m, rows_out,
              held, sem):
    core = core_ref[0]
    weights = weight_copies(core, own, oth, held, sem.at[0], 0, 3)
    cross = weight_copies(core, own, oth, held.at[pl.ds(3, 2)], sem.at[1], 5, 2)
    normed, factor = normalise(x_ref[...].astype(WIDE))
    wait_all(weights)
    grad_in = nt(dq[...], block(held, 0)) + nt(dk[...], block(held, 1)) + nt(dv[...], block(held, 2))
    grad, gain, bias = norm_back(grad_in, normed, factor, n_ref[0:1])
    back[...] = d_ref[...] + grad
    rows_out[...] = jnp.concatenate([gain, bias, jnp.zeros((6, D), WIDE)])
    wait_all(cross)
    back_m[...] = nt(dkc[...], block(held, 3)) + nt(dvc[...], block(held, 4))


SMALL = pl.BlockSpec(memory_space=pltpu.SMEM)
NEAR = pl.BlockSpec(memory_space=pltpu.VMEM)
FAR = pl.BlockSpec(memory_space=pl.ANY)
DMA = pltpu.SemaphoreType.DMA


def shape(*dims, dtype=LOW):
    return jax.ShapeDtypeStruct(dims, dtype)


def call(kernel, ins, outs, scratch, flops, name):
    return pl.pallas_call(
        kernel,
        in_specs=ins,
        out_specs=[spec for spec, _ in outs],
        out_shape=[form for _, form in outs],
        scratch_shapes=scratch,
        name=name,
        compiler_params=pltpu.CompilerParams(vmem_limit_bytes=56 * 2**20),
        cost_estimate=pl.CostEstimate(flops=flops, bytes_accessed=8 * 2**20, transcendentals=0),
    )


TOKENS = (NEAR, shape(TOK, D))
TOKENS_WIDE = (NEAR, shape(TOK, D, dtype=WIDE))
PROBS = (NEAR, shape(16, LEN, LEN))
MIXED = (NEAR, shape(2, D, LEN))
LINES = (NEAR, shape(8, D, dtype=WIDE))
HALF = (FAR, shape(4, 4, 64, D))
FULL = (FAR, shape(4, 8, 64, D))


def held(count):
    return pltpu.VMEM((count, 4, 2, 64, D), LOW)


def grads(count):
    return pltpu.VMEM((2, 4, count, 64, D), LOW)


run_self_forward = call(
    self_forward, [SMALL, NEAR, FAR, FAR],
    [TOKENS, TOKENS, TOKENS, PROBS, MIXED, TOKENS_WIDE, LINES],
    [held(4), pltpu.VMEM((8, 16, D), LOW), DMA((2,))], 2 * 7 * 10**8, "self_forward")
run_cross_forward = call(
    cross_forward, [SMALL, NEAR, NEAR, NEAR, FAR, FAR],
    [TOKENS, TOKENS, TOKENS, PROBS, MIXED, TOKENS_WIDE],
    [held(4), DMA((1,))], 2 * 7 * 10**8, "cross_forward")
run_feed_both = call(
    feed_both, [SMALL, NEAR, NEAR, NEAR, FAR, FAR],
    [TOKENS, TOKENS_WIDE, FULL, FULL, LINES],
    [held(4), held(4), grads(8), DMA((10,))], 2 * 33 * 10**8, "feed_both")
run_cross_back = call(
    cross_back, [SMALL, NEAR, NEAR, NEAR, NEAR, FAR, FAR] + [NEAR] * 5,
    [TOKENS_WIDE, TOKENS, TOKENS, HALF, HALF, LINES],
    [held(4), pltpu.VMEM((TOK, D), LOW), pltpu.VMEM((TOK, D), LOW), grads(4), DMA((3,))],
    2 * 12 * 10**8, "cross_back")
run_self_back = call(
    self_back, [SMALL, NEAR, NEAR, NEAR, FAR, FAR] + [NEAR] * 5,
    [TOKENS, TOKENS, TOKENS, HALF, HALF],
    [held(1), pltpu.VMEM((TOK, D), LOW), grads(4), DMA((3,))], 2 * 12 * 10**8, "self_back")
run_last_back = call(
    last_back, [SMALL, NEAR, NEAR, NEAR, FAR, FAR] + [NEAR] * 5,
    [TOKENS_WIDE, TOKENS_WIDE, LINES],
    [held(5), DMA((2,))], 2 * 7 * 10**8, "last_back")


STEP = 10
BETA_ONE = 0.9
BETA_TWO = 0.98
RATE = 0.1
RATE_NORM = 0.4
DECAY = 0.01
EPS_ADAM = 1e-09
SHARD = 64
FSDP = ("xlo", "z", "y", "core")


def exchange(part, axis):
    return lax.ppermute(part, axis, [(0, 1), (1, 0)])


def spread(part, axis, count):
    return lax.all_to_all(
        jnp.broadcast_to(part[None], (count,) + part.shape), axis, 0, 0, tiled=True
    )


def summed(part, axis):
    return lax.all_to_all(part, axis, 0, 0, tiled=True).astype(WIDE).sum(0)


def both(own, other):
    return (own.astype(WIDE) + other.astype(WIDE)).astype(LOW)


def gather_parameters(shard_w, shard_n):
    along_x = lax.axis_index("xlo")
    place = lax.axis_index(FSDP)
    lines = lax.dynamic_update_slice(jnp.zeros((16, D), LOW), shard_n, (0, place * 4))
    own = jnp.concatenate([shard_w, lines])
    other = exchange(own, "xlo")
    lines = own[SHARD:] + other[SHARD:]
    attn = jnp.where(along_x == 0, own[:SHARD], other[:SHARD])
    feed = jnp.where(along_x == 0, other[:SHARD], own[:SHARD])
    attn_z = spread(jnp.concatenate([attn, lines]), "z", 8)
    attn_z, feed = lax.optimization_barrier((attn_z, feed))
    feed_z = spread(feed, "z", 8)
    lines = attn_z[:, SHARD:].sum(0)
    attn_y = spread(jnp.concatenate([attn_z[:, :SHARD].reshape(8 * SHARD, D), lines]), "y", 4)
    attn_c = exchange(attn_y, "core")
    feed_y = spread(feed_z.reshape(8 * SHARD, D), "y", 4)
    feed_c = exchange(feed_y, "core")
    return attn_y, attn_c, feed_y, feed_c


def adam_update(param, first, second, grad, rate):
    first_new = BETA_ONE * first + (1.0 - BETA_ONE) * grad
    second_new = BETA_TWO * second + (1.0 - BETA_TWO) * grad * grad
    fix_one = 1.0 - BETA_ONE**STEP
    fix_two = 1.0 - BETA_TWO**STEP
    update = first_new / fix_one / (jnp.sqrt(second_new / fix_two) + EPS_ADAM)
    return (param - rate * (update + DECAY * param), second_new)


def local(
    inputs, memory, out_grad, weights, first_moment, second_moment, norms, norm_first, norm_second
):
    core = lax.axis_index("core").astype(jnp.int32).reshape(1)
    x, m, g = (part.reshape(TOK, D) for part in (inputs, memory, out_grad))
    own_a, oth_a, own_f, oth_f = gather_parameters(weights.astype(LOW), norms.astype(LOW))
    *kept_one, after_one, rows = run_self_forward(core, x, own_a, oth_a)
    *kept_two, after_two = run_cross_forward(core, after_one, m, rows, own_a, oth_a)
    result, grad_two, keep, sent, lines_three = run_feed_both(
        core, after_two, g, rows, own_f, oth_f
    )
    feed = both(keep, exchange(sent, "core"))
    grad_one, grad_kc, grad_vc, keep, sent, lines_two = run_cross_back(
        core, grad_two, after_one, m, rows, own_a, oth_a, *kept_two
    )
    cross = both(keep, exchange(sent, "core"))
    feed = summed(feed, "y")
    grad_q, grad_k, grad_v, keep, sent = run_self_back(
        core, grad_one, x, rows, own_a, oth_a, *kept_one
    )
    own = both(keep, exchange(sent, "core"))
    cross = summed(cross, "y")
    feed = summed(feed.astype(LOW), "z")
    grad_start, grad_memory, lines_one = run_last_back(
        core, grad_one, x, rows, own_a, oth_a, grad_q, grad_k, grad_v, grad_kc, grad_vc
    )
    lines = jnp.concatenate(
        [lines_one[:2], lines_two[:2], lines_three[:2], jnp.zeros((10, D), WIDE)]
    ).astype(LOW)
    lines = both(lines, exchange(lines, "core"))
    own = summed(own, "y")
    lines = lax.all_to_all(
        jnp.broadcast_to(lines[None], (4, 16, D)), "y", 0, 0, tiled=True
    ).astype(WIDE).sum(0).astype(LOW)
    attn = jnp.concatenate([own, cross], axis=0).astype(LOW)
    attn = jnp.concatenate([attn, jnp.broadcast_to(lines[None], (8, 16, D))], axis=1)
    attn = summed(attn, "z").astype(LOW)
    feed = jnp.concatenate([feed.astype(LOW), attn[SHARD:]])
    last = summed(jnp.stack([attn, feed, attn, feed]), ("xhi", "xlo"))
    owned_w = last[:SHARD]
    place = lax.axis_index(FSDP)
    owned_n = lax.dynamic_slice(last[SHARD : SHARD + 6], (0, place * 4), (6, 4))
    new_w, second_w = adam_update(weights, first_moment, second_moment, owned_w, RATE)
    new_n, second_n = adam_update(norms, norm_first, norm_second, owned_n, RATE_NORM)
    return (
        result.reshape(inputs.shape),
        grad_start.reshape(inputs.shape),
        grad_memory.reshape(inputs.shape),
        owned_w,
        new_w,
        second_w,
        owned_n,
        new_n,
        second_n,
    )


def solution(mesh):
    torus = jax.sharding.Mesh(mesh.devices.reshape(2, 8, 4, 2, 2), FSDP + ("xhi",))
    sentences = P(FSDP + ("xhi",), None, None)
    rows = P(FSDP, None)
    columns = P(None, FSDP)
    return jax.shard_map(
        local,
        mesh=torus,
        in_specs=(sentences,) * 3 + (rows,) * 3 + (columns,) * 3,
        out_specs=(sentences,) * 3 + (rows,) * 3 + (columns,) * 3,
        check_vma=False,
    )
```

```python
import jax
import jax.numpy as jnp
from jax import lax
from jax.experimental import pallas as pl
from jax.experimental.pallas import tpu as pltpu
from jax.sharding import PartitionSpec as P

LOW = jnp.bfloat16
WIDE = jnp.float32
HEADS = 8
HEAD = 64
LEN = 256
D = 512
FF = 2048
TOK = 512
EPS_NORM = 1e-05


def dot(former, latter, left, right):
    return lax.dot_general(
        former, latter, (((left,), (right,)), ((), ())), preferred_element_type=WIDE
    )


def nn(former, latter):
    return dot(former, latter, 1, 0)


def nt(former, latter):
    return dot(former, latter, 1, 1)


def tn(former, latter):
    return dot(former, latter, 0, 0)


def normalise(vector):
    centre = vector - jnp.mean(vector, axis=-1, keepdims=True)
    factor = lax.rsqrt(jnp.mean(centre * centre, axis=-1, keepdims=True) + EPS_NORM)
    return centre * factor, factor


def norm_back(grad, normed, factor, gain):
    scaled = grad * gain
    mean_one = jnp.mean(scaled, axis=-1, keepdims=True)
    mean_two = jnp.mean(scaled * normed, axis=-1, keepdims=True)
    return (
        factor * (scaled - mean_one - normed * mean_two),
        jnp.sum(grad * normed, axis=0, keepdims=True),
        jnp.sum(grad, axis=0, keepdims=True),
    )


def half_mask(which):
    lane = lax.broadcasted_iota(jnp.int32, (LEN, 128), 1)
    return (lane >= 64) if which else (lane < 64)


GROUP = 4
PLACES = [(s, pair, j) for s in range(2) for pair in range(4) for j in range(2)]


def window(s, pair):
    return pl.ds(s * LEN, LEN), pl.ds(pair * 128, 128)


def attend(q, k, v, prob, mixed, ended):
    masks = [half_mask(0), half_mask(1)]
    zero = jnp.zeros((LEN, 128), LOW)

    def scores(first):
        found = []
        for s, pair, j in PLACES[first : first + GROUP]:
            here = window(s, pair)
            found.append(nt(jnp.where(masks[j], k[here], zero), q[here]))
        return found

    def softmax(score):
        raised = jnp.exp(score - jnp.max(score, axis=0, keepdims=True))
        return (raised * (1.0 / jnp.sum(raised, axis=0, keepdims=True))).astype(LOW)

    ahead = scores(0)
    for first in range(0, 16, GROUP):
        current = ahead
        if first + GROUP < 16:
            ahead = scores(first + GROUP)
        softs = [softmax(score) for score in current]
        for i, (s, pair, j) in enumerate(PLACES[first : first + GROUP]):
            prob[first + i] = softs[i]
            values = v[window(s, pair)].T[j * 64 : (j + 1) * 64]
            mixed[s, pl.ds(pair * 128 + j * 64, 64)] = nn(values, softs[i]).astype(LOW)
        if first + GROUP in (8, 16):
            ended(first // 8)


def attend_back(q, k, v, prob, go, dq, dk, dv):
    masks = [half_mask(0), half_mask(1)]
    zero = jnp.zeros((LEN, 128), LOW)

    def grad_softs(first):
        found = []
        for s, pair, j in PLACES[first : first + GROUP]:
            here = window(s, pair)
            found.append(nt(jnp.where(masks[j], v[here], zero), go[here]))
        return found

    def grad_score(place, grad_soft):
        soft = prob[place].astype(WIDE)
        weighed = soft * grad_soft
        return (weighed - soft * jnp.sum(weighed, axis=0, keepdims=True)).astype(LOW)

    ahead = grad_softs(0)
    for first in range(0, 16, GROUP):
        current = ahead
        if first + GROUP < 16:
            ahead = grad_softs(first + GROUP)
        grads = [grad_score(first + i, part) for i, part in enumerate(current)]
        for i in range(0, GROUP, 2):
            s, pair, _ = PLACES[first + i]
            here = window(s, pair)
            one, two = grads[i], grads[i + 1]
            out, queries, keys = go[here], q[here], k[here].T
            dv[here] = jnp.where(
                masks[0], nn(prob[first + i], out), nn(prob[first + i + 1], out)
            ).astype(LOW)
            dk[here] = jnp.where(masks[0], nn(one, queries), nn(two, queries)).astype(LOW)
            grad_q = jnp.concatenate([nn(keys[:64], one), nn(keys[64:], two)], axis=0)
            dq[here] = (grad_q * HEAD ** (-0.5)).astype(LOW).T


class Moves:
    def __init__(self, sem):
        self.sem, self.used = sem, 0

    def start(self, *pairs):
        copies = [
            pltpu.make_async_copy(source, target, self.sem.at[self.used])
            for source, target in pairs
        ]
        self.used += 1
        for copy in copies:
            copy.start()
        return copies


def wait(*groups):
    for group in groups:
        for copy in group:
            copy.wait()


def attn_pieces(at, own, oth, held, first, slot, count=1):
    return [
        (
            source.at[lax.rem(at[1] - line + 4, 4), pl.ds((first + b) * 64, 64)],
            held.at[slot + b, line, place],
        )
        for place, source in ((at[2], own), (1 - at[2], oth))
        for line in range(4)
        for b in range(count)
    ]


def feed_pieces(at, whole, held, b):
    return [
        (whole.at[b, :, lax.rem(at[1] - line + 4, 4)], held.at[b, line]) for line in range(4)
    ]


def block(held, b):
    return held[b].reshape(D, D)


def self_forward(at, x_far, own, oth, q_far, k_far, v_far, prob_far, mixed_far, norms,
                 x, q, k, v, prob, mixed, held, pieces, sem):
    moves = Moves(sem)
    got_x = moves.start((x_far, x))
    got_pieces = moves.start(
        *[
            (source.at[slot, pl.ds(192, 16)], pieces.at[place * 4 + slot])
            for place, source in ((0, own), (1, oth))
            for slot in range(4)
        ]
    )
    got_w = [moves.start(*attn_pieces(at, own, oth, held, b, b)) for b in range(3)]
    wait(got_x)
    normed, _ = normalise(x[...].astype(WIDE))
    wait(got_pieces)
    rows = jnp.sum(pieces[...].astype(WIDE), axis=0)
    norms[...] = rows[:8]
    first_in = (normed * rows[0:1] + rows[1:2]).astype(LOW)
    wait(*got_w)
    q[...] = nn(first_in, block(held, 0)).astype(LOW) * LOW(HEAD ** (-0.5))
    k[...] = nn(first_in, block(held, 1)).astype(LOW)
    v[...] = nn(first_in, block(held, 2)).astype(LOW)
    out = [moves.start((q, q_far)), moves.start((k, k_far)), moves.start((v, v_far))]

    def ended(s):
        heads = pl.ds(s * 8, 8)
        out.append(moves.start((prob.at[heads], prob_far.at[heads])))
        out.append(moves.start((mixed.at[s], mixed_far.at[s])))

    attend(q, k, v, prob, mixed, ended)
    wait(*out)


def cross_forward(at, x_far, m_far, n_ref, first_far, own, oth,
                  q_far, k_far, v_far, prob_far, mixed_far, between_far, after_far,
                  x, m, first, q, k, v, prob, mixed, between, after, held, sem):
    moves = Moves(sem)
    got_m = moves.start((m_far, m))
    got_kv = moves.start(*attn_pieces(at, own, oth, held, 2, 2, 2))
    got_x = moves.start((x_far, x), (first_far, first))
    got_o = moves.start(*attn_pieces(at, own, oth, held, 0, 0, 2))
    got_last = moves.start(*attn_pieces(at, own, oth, held, 4, 4))
    wait(got_m, got_kv)
    k[...] = nn(m[...], block(held, 2)).astype(LOW)
    v[...] = nn(m[...], block(held, 3)).astype(LOW)
    out = [moves.start((k, k_far)), moves.start((v, v_far))]
    wait(got_x, got_o)
    for s in range(2):
        lines = pl.ds(s * LEN, LEN)
        between[lines, :] = x[lines, :].astype(WIDE) + tn(first[s], block(held, 0))
    out.append(moves.start((between, between_far)))
    normed, _ = normalise(between[...])
    second_in = (normed * n_ref[2:3] + n_ref[3:4]).astype(LOW)
    q[...] = nn(second_in, block(held, 1)).astype(LOW) * LOW(HEAD ** (-0.5))
    out.append(moves.start((q, q_far)))

    def ended(s):
        heads = pl.ds(s * 8, 8)
        out.append(moves.start((prob.at[heads], prob_far.at[heads])))
        out.append(moves.start((mixed.at[s], mixed_far.at[s])))

    attend(q, k, v, prob, mixed, ended)
    wait(got_last)
    for s in range(2):
        lines = pl.ds(s * LEN, LEN)
        after[lines, :] = between[lines, :] + tn(mixed[s], block(held, 4))
        out.append(moves.start((after.at[lines], after_far.at[lines])))
    wait(*out)


def store_grad(grads, at, b, value):
    parts = value.astype(LOW).reshape(4, 2, 64, D)
    for line in range(4):
        slot = lax.rem(line - at[1] + 4, 4)
        for core in range(2):
            grads[lax.rem(core + at[2], 2), slot, b] = parts[line, core]


def feed_both(at, x_far, g_far, n_ref, whole, result_far, back_far, grads_far, rows_out,
              x, g, result, back, held, grads, sem):
    moves = Moves(sem)
    got_x = moves.start((x_far, x))
    got = {}
    for b in (0, 4, 1, 5, 2, 6, 3, 7):
        got[b] = moves.start(*feed_pieces(at, whole, held, b))
        if b == 0:
            got_g = moves.start((g_far, g))
    out = []

    def store(b, value):
        parts = value.astype(LOW).reshape(4, 2, 64, D)
        for line in range(4):
            slot = lax.rem(line - at[1] + 4, 4)
            for core in range(2):
                grads[b, core, slot] = parts[line, core]
        out.append(moves.start((grads.at[b], grads_far.at[b])))

    wait(got_x)
    normed, factor = normalise(x[...])
    third_in = (normed * n_ref[4:5] + n_ref[5:6]).astype(LOW)

    def products(c):
        wait(got[c], got[4 + c])
        return nt(third_in, block(held, c)), nt(g[...], block(held, 4 + c))

    wait(got_g)
    ahead = products(0)
    forward = grad_in = None
    for c in range(4):
        up, grad_act = ahead
        if c < 3:
            ahead = products(c + 1)
        sigma = 1.0 / (1.0 + jnp.exp(-up))
        active = up * sigma
        grad_up = (grad_act * (sigma + active * (1.0 - sigma))).astype(LOW)
        active = active.astype(LOW)
        part = nn(grad_up, block(held, c))
        grad_in = part if grad_in is None else grad_in + part
        store(c, tn(grad_up, third_in))
        store(4 + c, tn(active, g[...]))
        part = nn(active, block(held, 4 + c))
        forward = part if forward is None else forward + part
    grad, gain, bias = norm_back(grad_in, normed, factor, n_ref[4:5])
    back[...] = g[...].astype(WIDE) + grad
    out.append(moves.start((back, back_far)))
    result[...] = (x[...] + forward).astype(LOW)
    out.append(moves.start((result, result_far)))
    rows_out[...] = jnp.concatenate([jnp.zeros((4, D), WIDE), gain, bias, jnp.zeros((2, D), WIDE)])
    wait(*out)


def cross_back(at, d_far, x_far, m_far, n_ref, lines, own, oth,
               q_far, k_far, v_far, prob_far, mixed_far,
               back_far, dk_far, dv_far, kept, sent, rows_out,
               d, x, m, q, k, v, prob, mixed, back, dk, dv, held, go, dq, grads, sem):
    moves = Moves(sem)
    got_d = moves.start((d_far, d))
    got_o = moves.start(*attn_pieces(at, own, oth, held, 4, 3))
    got_v = moves.start((v_far, v), (prob_far, prob))
    got_mixed = moves.start((mixed_far, mixed))
    got_qk = moves.start((q_far, q), (k_far, k))
    got_x = moves.start((x_far, x), (m_far, m))
    got_q = moves.start(*attn_pieces(at, own, oth, held, 1, 0))
    out = []

    def store(b, value):
        store_grad(grads, at, b, value)
        out.append(moves.start((grads.at[0, :, b], kept.at[:, b]), (grads.at[1, :, b], sent.at[:, b])))

    wait(got_d)
    down = d[...].astype(LOW)
    wait(got_o)
    go[...] = nt(down, block(held, 3)).astype(LOW)
    wait(got_mixed)
    store(3, nn(mixed[0], down[:LEN]) + nn(mixed[1], down[LEN:]))
    wait(got_v, got_qk)
    attend_back(q, k, v, prob, go, dq, dk, dv)
    out.append(moves.start((dk, dk_far), (dv, dv_far)))
    wait(got_x, got_q)
    store(1, tn(m[...], dk[...]))
    store(2, tn(m[...], dv[...]))
    grad_in = nt(dq[...], block(held, 0))
    normed, factor = normalise(x[...])
    second_in = (normed * n_ref[2:3] + n_ref[3:4]).astype(LOW)
    store(0, tn(second_in, dq[...]))
    grad, gain, bias = norm_back(grad_in, normed, factor, n_ref[2:3])
    back[...] = d[...] + grad
    out.append(moves.start((back, back_far)))
    rows_out[...] = jnp.concatenate([lines[0:2], gain, bias, lines[4:8]])
    wait(*out)


def self_back(at, d_far, x_far, n_ref, own, oth, q_far, k_far, v_far, prob_far, mixed_far,
              dq_far, dk_far, dv_far, kept, sent,
              d, x, q, k, v, prob, mixed, dq, dk, dv, held, go, grads, sem):
    moves = Moves(sem)
    got_d = moves.start((d_far, d))
    got_o = moves.start(*attn_pieces(at, own, oth, held, 0, 0))
    got_v = moves.start((v_far, v), (prob_far, prob))
    got_mixed = moves.start((mixed_far, mixed))
    got_qk = moves.start((q_far, q), (k_far, k))
    got_x = moves.start((x_far, x))
    out = []

    def store(b, value):
        store_grad(grads, at, b, value)
        out.append(moves.start((grads.at[0, :, b], kept.at[:, b]), (grads.at[1, :, b], sent.at[:, b])))

    wait(got_d)
    down = d[...].astype(LOW)
    wait(got_o)
    go[...] = nt(down, block(held, 0)).astype(LOW)
    wait(got_mixed)
    store(3, nn(mixed[0], down[:LEN]) + nn(mixed[1], down[LEN:]))
    wait(got_x)
    normed, _ = normalise(x[...].astype(WIDE))
    first_in = (normed * n_ref[0:1] + n_ref[1:2]).astype(LOW)
    wait(got_v, got_qk)
    attend_back(q, k, v, prob, go, dq, dk, dv)
    store(0, tn(first_in, dq[...]))
    store(1, tn(first_in, dk[...]))
    store(2, tn(first_in, dv[...]))
    out.append(moves.start((dq, dq_far), (dk, dk_far), (dv, dv_far)))
    wait(*out)


def last_back(at, d_far, x_far, n_ref, lines, own, oth, own_r, oth_r,
              dq_far, dk_far, dv_far, dkc_far, dvc_far, back_far, back_m_far, rows_out,
              d, x, dq, dk, dv, dkc, dvc, back, back_m, held, sem):
    moves = Moves(sem)
    got_s = moves.start((dq_far, dq), (dk_far, dk), (dv_far, dv))
    got_w = moves.start(*attn_pieces(at, own, oth, held, 0, 0, 3))
    got_x = moves.start((x_far, x), (d_far, d))
    got_c = moves.start((dkc_far, dkc), (dvc_far, dvc))
    got_wc = moves.start(*attn_pieces(at, own_r, oth_r, held, 2, 3, 2))
    wait(got_s, got_w)
    grad_in = nt(dq[...], block(held, 0)) + nt(dk[...], block(held, 1)) + nt(dv[...], block(held, 2))
    wait(got_x)
    normed, factor = normalise(x[...].astype(WIDE))
    grad, gain, bias = norm_back(grad_in, normed, factor, n_ref[0:1])
    back[...] = d[...] + grad
    out = [moves.start((back, back_far))]
    rows = jnp.concatenate([gain, bias, lines[2:8], jnp.zeros((8, D), WIDE)])
    rows_out[...] = rows.astype(LOW)
    wait(got_c, got_wc)
    back_m[...] = nt(dkc[...], block(held, 3)) + nt(dvc[...], block(held, 4))
    out.append(moves.start((back_m, back_m_far)))
    wait(*out)


SMALL = pl.BlockSpec(memory_space=pltpu.SMEM)
NEAR = pl.BlockSpec(memory_space=pltpu.VMEM)
FAR = pl.BlockSpec(memory_space=pltpu.HBM)


def shape(*dims, dtype=LOW):
    return jax.ShapeDtypeStruct(dims, dtype)


def call(kernel, ins, outs, scratch, sems, flops, name):
    return pl.pallas_call(
        kernel,
        in_specs=ins,
        out_specs=[spec for spec, _ in outs],
        out_shape=[form for _, form in outs],
        scratch_shapes=scratch + [pltpu.SemaphoreType.DMA((sems,))],
        name=name,
        compiler_params=pltpu.CompilerParams(vmem_limit_bytes=56 * 2**20),
        cost_estimate=pl.CostEstimate(flops=flops, bytes_accessed=8 * 2**20, transcendentals=0),
    )


LINES = (NEAR, shape(8, D, dtype=WIDE))
HALF = (FAR, shape(4, 4, 64, D))
FULL = (FAR, shape(8, 2, 4, 64, D))
TOKENS = pltpu.VMEM((TOK, D), LOW)
WIDES = pltpu.VMEM((TOK, D), WIDE)
PROBS = pltpu.VMEM((16, LEN, LEN), LOW)
MIXED = pltpu.VMEM((2, D, LEN), LOW)
HELD = pltpu.VMEM((8, 4, 2, 64, D), LOW)
GRADS = pltpu.VMEM((2, 4, 4, 64, D), LOW)


def far(scratch):
    return FAR, shape(*scratch.shape, dtype=scratch.dtype)


run_self_forward = call(
    self_forward, [SMALL] + [FAR] * 3,
    [far(TOKENS)] * 3 + [far(PROBS), far(MIXED), LINES],
    [TOKENS] * 4 + [PROBS, MIXED, HELD, pltpu.VMEM((8, 16, D), LOW)],
    12, 2 * 6 * 10**8, "self_forward")
run_cross_forward = call(
    cross_forward, [SMALL, FAR, FAR, NEAR] + [FAR] * 3,
    [far(TOKENS)] * 3 + [far(PROBS), far(MIXED), far(WIDES), far(WIDES)],
    [TOKENS, TOKENS, MIXED] + [TOKENS] * 3 + [PROBS, MIXED, WIDES, WIDES, HELD],
    16, 2 * 8 * 10**8, "cross_forward")
run_feed_both = call(
    feed_both, [SMALL, FAR, FAR, NEAR, FAR],
    [far(TOKENS), far(WIDES), FULL, LINES],
    [WIDES, TOKENS, TOKENS, WIDES, HELD, pltpu.VMEM((8, 2, 4, 64, D), LOW)],
    20, 2 * 33 * 10**8, "feed_both")
run_cross_back = call(
    cross_back, [SMALL, FAR, FAR, FAR, NEAR, NEAR] + [FAR] * 7,
    [far(WIDES), far(TOKENS), far(TOKENS), HALF, HALF, LINES],
    [WIDES, WIDES, TOKENS] + [TOKENS] * 3 + [PROBS, MIXED, WIDES, TOKENS, TOKENS, HELD, TOKENS,
                                             TOKENS, GRADS],
    14, 2 * 12 * 10**8, "cross_back")
run_self_back = call(
    self_back, [SMALL, FAR, FAR, NEAR] + [FAR] * 7,
    [far(TOKENS)] * 3 + [HALF, HALF],
    [WIDES, TOKENS] + [TOKENS] * 3 + [PROBS, MIXED] + [TOKENS] * 3 + [HELD, TOKENS, GRADS],
    12, 2 * 12 * 10**8, "self_back")
run_last_back = call(
    last_back, [SMALL, FAR, FAR, NEAR, NEAR] + [FAR] * 9,
    [far(WIDES), far(WIDES), (NEAR, shape(16, D))],
    [WIDES, TOKENS] + [TOKENS] * 5 + [WIDES, WIDES, HELD],
    8, 2 * 7 * 10**8, "last_back")


STEP = 10
BETA_ONE = 0.9
BETA_TWO = 0.98
RATE = 0.1
RATE_NORM = 0.4
DECAY = 0.01
EPS_ADAM = 1e-09
SHARD = 64
FSDP = ("xlo", "z", "y", "core")


def shift(part, axis, count, step):
    return lax.ppermute(part, axis, [(i, (i + step) % count) for i in range(count)])


def exchange(part, axis):
    return shift(part, axis, 2, 1)


def both(own, other):
    return (own.astype(WIDE) + other.astype(WIDE)).astype(LOW)


def total(parts):
    return sum(part.astype(WIDE) for part in parts)


def along_y(part):
    return [part] + [shift(part, "y", 4, j) for j in (1, 2, 3)]


def across_y(parts):
    return total([parts[0]] + [shift(parts[j], "y", 4, j) for j in (1, 2, 3)])


def gather_parameters(shard_w, shard_n):
    along_x = lax.axis_index("xlo")
    place = lax.axis_index(FSDP)
    lines = lax.dynamic_update_slice(jnp.zeros((16, D), LOW), shard_n, (0, place * 4))
    own = jnp.concatenate([shard_w, lines])
    other = exchange(own, "xlo")
    lines = own[SHARD:] + other[SHARD:]
    attn = jnp.concatenate([jnp.where(along_x == 0, own[:SHARD], other[:SHARD]), lines])
    feed = jnp.concatenate(along_y(jnp.where(along_x == 0, other[:SHARD], own[:SHARD])))
    attn = lax.all_to_all(jnp.broadcast_to(attn[None], (8, 80, D)), "z", 0, 0, tiled=True)
    feed, attn = lax.optimization_barrier((feed, attn))
    feed = lax.all_gather(feed, ("z", "core"), axis=0, tiled=True)
    first = jnp.concatenate([attn[:3, :SHARD].reshape(192, D), attn[:, SHARD:].sum(0)])
    first = jnp.concatenate(along_y(first)).reshape(4, 208, D)
    first_other = exchange(first, "core")
    rest, first_other = lax.optimization_barrier((attn[3:, :SHARD].reshape(320, D), first_other))
    return first, first_other, along_y(rest), feed.reshape(8, 2, 4, SHARD, D)


def adam_update(param, first, second, grad, rate):
    first_new = BETA_ONE * first + (1.0 - BETA_ONE) * grad
    second_new = BETA_TWO * second + (1.0 - BETA_TWO) * grad * grad
    fix_one = 1.0 - BETA_ONE**STEP
    fix_two = 1.0 - BETA_TWO**STEP
    update = first_new / fix_one / (jnp.sqrt(second_new / fix_two) + EPS_ADAM)
    return (param - rate * (update + DECAY * param), second_new)


def local(
    inputs, memory, out_grad, weights, first_moment, second_moment, norms, norm_first, norm_second
):
    at = jnp.stack([lax.axis_index(axis) for axis in ("z", "y", "core")]).astype(jnp.int32)
    x, m, g = (part.reshape(TOK, D) for part in (inputs, memory, out_grad))
    own_a, oth_a, rest, feed = gather_parameters(weights.astype(LOW), norms.T.astype(LOW).T)
    *kept_one, rows = run_self_forward(at, x, own_a, oth_a)
    *rest, mixed = lax.optimization_barrier((*rest, kept_one[-1]))
    own_r = jnp.concatenate(rest).reshape(4, 320, D)
    oth_r = exchange(own_r, "core")
    *kept_two, after_one, after_two = run_cross_forward(at, x, m, rows, mixed, own_r, oth_r)
    result, grad_two, feed, lines = run_feed_both(at, after_two, g, rows, feed)
    feed = lax.psum_scatter(
        feed.reshape(16, 256, D), ("z", "core"), scatter_dimension=0, tiled=False
    ).reshape(4, SHARD, D)
    grad_one, grad_kc, grad_vc, keep_two, sent, lines = run_cross_back(
        at, grad_two, after_one, m, rows, lines, own_r, oth_r, *kept_two
    )
    other_two = exchange(sent, "core")
    grad_q, grad_k, grad_v, keep, sent = run_self_back(
        at, grad_one, x, rows, own_r, oth_r, *kept_one
    )
    other = exchange(sent, "core")
    grad_start, grad_memory, lines = run_last_back(
        at, grad_one, x, rows, lines, own_a, oth_a, own_r, oth_r,
        grad_q, grad_k, grad_v, grad_kc, grad_vc,
    )
    first, *parts = [
        jnp.concatenate([both(keep[j], other[j]), both(keep_two[j], other_two[j])])
        for j in range(4)
    ]
    parts = [shift(part, "y", 4, j + 1) for j, part in enumerate(parts)]
    lines = both(lines, exchange(lines, "core"))
    parts[0], lines = lax.optimization_barrier((parts[0], lines))
    lines = across_y([lines] * 4).astype(LOW)
    attn = total([first] + parts).astype(LOW)
    attn = jnp.concatenate([attn, jnp.broadcast_to(lines[None], (8, 16, D))], axis=1)
    attn = lax.all_to_all(attn, "z", 0, 0, tiled=True)
    feed = across_y(feed).astype(LOW)
    feed, attn = lax.optimization_barrier((feed, attn))
    attn = total(attn).astype(LOW)
    along_x = lax.axis_index("xlo")
    mine = jnp.concatenate([jnp.where(along_x == 0, attn[:SHARD], feed), attn[SHARD:]])
    rest = jnp.concatenate([jnp.where(along_x == 0, feed, attn[:SHARD]), attn[SHARD:]])
    cross_x = lax.ppermute(rest, ("xlo", "xhi"), [(i, 3 - i) for i in range(4)])
    last = total([mine, exchange(rest, "xlo"), exchange(mine, "xhi"), cross_x])
    owned_w = last[:SHARD]
    place = lax.axis_index(FSDP)
    owned_n = lax.dynamic_slice(last[SHARD : SHARD + 6], (0, place * 4), (6, 4)).T
    new_w, second_w = adam_update(weights, first_moment, second_moment, owned_w, RATE)
    new_n, second_n = adam_update(norms.T, norm_first.T, norm_second.T, owned_n, RATE_NORM)
    return (
        result.reshape(inputs.shape),
        grad_start.reshape(inputs.shape),
        grad_memory.reshape(inputs.shape),
        owned_w,
        new_w,
        second_w,
        owned_n.T,
        new_n.T,
        second_n.T,
    )


def solution(mesh):
    torus = jax.sharding.Mesh(mesh.devices.reshape(2, 8, 4, 2, 2), FSDP + ("xhi",))
    sentences = P(FSDP + ("xhi",), None, None)
    rows = P(FSDP, None)
    columns = P(None, FSDP)
    return jax.shard_map(
        local,
        mesh=torus,
        in_specs=(sentences,) * 3 + (rows,) * 3 + (columns,) * 3,
        out_specs=(sentences,) * 3 + (rows,) * 3 + (columns,) * 3,
        check_vma=False,
    )
```
